256 devices in a mesh: frames: 16 (over x, y_hi, core), tmpl: 16 (over y_lo, z).
Axes of the slice: x: 4, y: 4 (y_hi: 2, y_lo: 2; y = y_hi * 2 + y_lo), z: 8, core: 2. Of those that a mesh axis runs over, the one named last changes fastest.
Arguments:
- frames: bfloat16 [5120, 64, 128], P(('frames', 'tmpl')), may hold values from -15 to 15
- lengths: int32 [5120], P(('frames', 'tmpl')), may hold values from 8 to 64
- templates: bfloat16 [4096, 64, 128], P(('frames', 'tmpl')), may hold values from -8 to 8
- bin_ids: int32 [4096], P(('frames', 'tmpl')), may hold values from 0 to 1023
- harmonics: float32 [1024, 512], replicated, may hold values from -6 to 6
Outputs:
- coefficients: float32 [5120, 512], P(('frames', 'tmpl'))
- rotation_posterior: float32 [5120, 128], P(('frames', 'tmpl'))
The draws below stay inside these ranges and needn't reach their ends.
All inputs are finite; a program needn't handle non-finite values.
Results may differ from the reference program's by a relative error of at most 0.0039.
The reference program's roundings to bfloat16 on the way count: a program that leaves them out, or rounds other values in their place, can miss the bound.
Values may be sent and summed in bfloat16 or wider, within the bound.
No kernel may reach another device: no remote copies, remote signals or barrier semaphores. Data moves between devices by JAX's collectives and lax.ppermute only.
A program may use at most 192 MiB of HBM per device.

```python
import math
import jax
import jax.numpy as jnp
from jax import lax

RADII = 64
HARMONICS = 64
ANGLES = 128
COEFS = 512
BINS = 1024
FRAMES = 5120
TEMPLATES = 4096


def common_lengths(key):
    subkey = jax.random.fold_in(key, 101)
    drawn = jax.random.randint(subkey, (FRAMES,), 8, RADII + 1)
    return drawn.at[0].set(RADII).at[1].set(8)


def base_templates(key):
    subkey = jax.random.fold_in(key, 202)
    return jnp.clip(jax.random.normal(subkey, (TEMPLATES, RADII, 2 * HARMONICS), jnp.float32), -5.0, 5.0)


def draw_lengths(key, part):
    return common_lengths(key)


def draw_templates(key, part):
    base = base_templates(key)
    return base.astype(jnp.bfloat16)


def draw_frames(key, part):
    key = jax.random.fold_in(key, 4)
    first = jax.random.fold_in(key, 0)
    entries = jnp.clip(jax.random.normal(first, (FRAMES, RADII, 2 * HARMONICS), jnp.float32), -5.0, 5.0)
    return entries.astype(jnp.bfloat16)


def with_ends(result, key, smallest, high):
    place = [jax.random.randint(jax.random.fold_in(key, axis), (), 0, length) for axis, length in enumerate(result.shape)]
    longest = result.shape.index(max(result.shape))
    next_to = place[:longest] + [(place[longest] + 1) % result.shape[longest]] + place[longest + 1:]
    return result.at[tuple(place)].set(smallest).at[tuple(next_to)].set(high)


def gaussian(rng, dims, width, reach, kind=jnp.bfloat16):
    return jnp.clip(width * jax.random.normal(rng, dims, jnp.float32), -reach, reach).astype(kind)


def setup_inputs(seed: int = 0) -> dict:
    key_of = jax.random.split(jax.random.key(seed), 6)
    frames = draw_frames(jax.random.fold_in(key_of[5], 71), 0)
    lengths = draw_lengths(jax.random.fold_in(key_of[5], 71), 0)
    templates = draw_templates(jax.random.fold_in(key_of[5], 71), 0)
    bin_ids = with_ends(jax.random.randint(key_of[3], (TEMPLATES,), 0, BINS), jax.random.fold_in(key_of[3], 1), 0, BINS - 1).astype(jnp.int32)
    harmonics = gaussian(key_of[4], (BINS, COEFS), 1.0, 6.0, jnp.float32)
    return dict(frames=frames, lengths=lengths, templates=templates, bin_ids=bin_ids, harmonics=harmonics)


def rotation_table():
    harmonic = lax.broadcasted_iota(jnp.int32, (HARMONICS, ANGLES), 0)
    angle_index = lax.broadcasted_iota(jnp.int32, (HARMONICS, ANGLES), 1)
    phases = (harmonic * angle_index % ANGLES).astype(jnp.float32) * (2.0 * math.pi / ANGLES)
    weight = jnp.where(harmonic == 0, 1.0, 2.0).astype(jnp.float32)
    return jnp.stack([weight * jnp.cos(phases), -weight * jnp.sin(phases)]).astype(jnp.bfloat16)

def radial_inputs(frames, lengths):
    radius = lax.broadcasted_iota(jnp.int32, (1, RADII, 1), 1)
    masked = jnp.where(radius < lengths[:, None, None], frames, jnp.zeros_like(frames))
    scaling = 1.0 / (8.0 * jnp.sqrt(lengths.astype(jnp.float32)))
    return (masked, scaling)

def split_columns(spectra):
    return jnp.concatenate([spectra[..., :HARMONICS], spectra[..., HARMONICS:]], axis=1)

def correlate(frame_rows, template_cat, rotation, scaling):
    real_part = frame_rows[..., :HARMONICS]
    imag_part = frame_rows[..., HARMONICS:]
    stacked = jnp.stack([jnp.concatenate([real_part, imag_part], 1), jnp.concatenate([imag_part, -real_part], 1)])
    cross = jnp.einsum('sfrm,trm->smft', stacked.astype(jnp.float32), template_cat).astype(jnp.bfloat16)
    scores = jnp.einsum('smft,smk->ftk', cross.astype(jnp.float32), rotation.astype(jnp.float32))
    return scores * scaling[:, None, None]

def reference(frames, lengths, templates, bin_ids, harmonics):
    masked, scaling = radial_inputs(frames, lengths)
    template_cat = split_columns(templates).astype(jnp.float32)
    projection = harmonics[bin_ids]
    rotation = rotation_table()
    count = FRAMES // 64

    def one_block(inputs):
        rows, scales = inputs
        scores = correlate(rows, template_cat, rotation, scales)
        highest = lax.optimization_barrier(jnp.max(scores, axis=(1, 2)))
        weights = jnp.exp(scores - highest[:, None, None])
        totals = lax.optimization_barrier(jnp.sum(weights, axis=(1, 2)))
        posterior = weights / totals[:, None, None]
        rotations = lax.optimization_barrier(jnp.sum(posterior, axis=1))
        per_template = lax.optimization_barrier(jnp.sum(posterior, axis=2))
        coefs = jnp.dot(per_template, projection, precision=lax.Precision.HIGHEST)
        return (coefs, rotations)
    coefs, rotations = lax.map(one_block, (masked.reshape(count, 64, RADII, 2 * HARMONICS), scaling.reshape(count, 64)))
    return (coefs.reshape(FRAMES, COEFS), rotations.reshape(FRAMES, ANGLES))
```

```python
import functools
import math

import jax
import jax.numpy as jnp
from jax import lax
from jax.experimental import pallas as pl
from jax.experimental.pallas import tpu as pltpu
from jax.sharding import PartitionSpec as P

RADII = 64
HARMONICS = 64
ANGLES = 128
COEFS = 512
BINS = 1024
WIDTH = 768
ROT = COEFS
TOT = COEFS + ANGLES
STRIDE = 129
LOG2E = math.log2(math.e)
AXES = ("frames", "tmpl")
VMEM = pl.BlockSpec(memory_space=pltpu.VMEM)
SMEM = pl.BlockSpec(memory_space=pltpu.SMEM)
CHIPS_X, CHIPS_Y, CHIPS_Z = 4, 4, 8


def device(x, y, z, core):
    return (((x * 2 + y // 2) * 2 + core) * 2 + y % 2) * CHIPS_Z + z


def move(value, step):
    pairs = []
    for x in range(CHIPS_X):
        for y in range(CHIPS_Y):
            for z in range(CHIPS_Z):
                for core in range(2):
                    dx, dy, dz, dc = step(core)
                    there = device((x + dx) % CHIPS_X, (y + dy) % CHIPS_Y, (z + dz) % CHIPS_Z, (core + dc) % 2)
                    pairs.append((device(x, y, z, core), there))
    return lax.ppermute(value, AXES, pairs)


def swap(value):
    return move(value, lambda core: (0, 0, 0, 1))


def along_z(value, steps):
    return move(value, lambda core: (0, 0, steps if core == 0 else -steps, 0))


def first_axis(value, steps):
    return move(value, lambda core: (steps, 0, 0, 0) if core == 0 else (0, steps, 0, 0))


def second_axis(value, steps):
    return move(value, lambda core: (0, steps, 0, 0) if core == 0 else (steps, 0, 0, 0))


def rotation_table():
    harmonic = lax.broadcasted_iota(jnp.int32, (HARMONICS, ANGLES), 0)
    angle_index = lax.broadcasted_iota(jnp.int32, (HARMONICS, ANGLES), 1)
    phases = (harmonic * angle_index % ANGLES).astype(jnp.float32) * (2.0 * math.pi / ANGLES)
    weight = jnp.where(harmonic == 0, 1.0, 2.0).astype(jnp.float32)
    table = jnp.concatenate([weight * jnp.cos(phases), -weight * jnp.sin(phases)], axis=0)
    return table.astype(jnp.bfloat16).T


def harmonic_rows(spectrum):
    turned = spectrum.T
    return jnp.concatenate([turned[:HARMONICS], turned[HARMONICS:]], axis=1)


def prepare_kernel(lengths, bins, frames, templates, raw, tmpl, scratch, rows):
    count = frames.shape[0]
    radius = lax.broadcasted_iota(jnp.int32, (RADII, 2 * HARMONICS), 0)
    rows[...] = jnp.zeros_like(rows)
    for f in range(count):
        raw[f] = jnp.where(radius < lengths[f], frames[f].astype(jnp.float32), 0.0).astype(jnp.bfloat16)
        rows[f : f + 1, :] = jnp.full((1, 128), lengths[f].astype(jnp.float32))
    raw[count] = rows[...].astype(jnp.bfloat16)
    size = templates.shape[0]
    for t in range(size):
        scratch[pl.ds(t, HARMONICS, stride=size + 1), :] = harmonic_rows(templates[t].astype(jnp.float32))
    for m in range(HARMONICS):
        tmpl[m] = scratch[pl.ds(m * (size + 1), size), :].astype(jnp.bfloat16)
    lane = lax.broadcasted_iota(jnp.int32, (1, 128), 1)
    for t in range(size):
        high, low = (bins[t] >> 5).astype(jnp.float32), (bins[t] & 31).astype(jnp.float32)
        rows[t : t + 1, :] = jnp.where(lane == 0, high, low)
    tmpl[HARMONICS] = rows[0:size, :].astype(jnp.bfloat16)


def prepare(lengths, bins, frames, templates):
    count, size = frames.shape[0], templates.shape[0]
    return pl.pallas_call(
        prepare_kernel,
        out_shape=(
            jax.ShapeDtypeStruct((count + 1, RADII, 128), jnp.bfloat16),
            jax.ShapeDtypeStruct((HARMONICS + 1, size, 128), jnp.bfloat16),
        ),
        in_specs=[SMEM, SMEM, VMEM, VMEM],
        out_specs=(VMEM, VMEM),
        scratch_shapes=[
            pltpu.VMEM((HARMONICS * (size + 1), 128), jnp.float32),
            pltpu.VMEM((RADII, 128), jnp.float32),
        ],
        name="prepare",
    )(lengths, bins, frames, templates)


def arrange_kernel(core, mine, theirs, out, scratch, rows):
    count = mine.shape[0] - 1
    both = 2 * count
    here = core[0] * count
    there = count - here
    for source, start in ((mine, here), (theirs, there)):
        for f in range(count):
            scratch[pl.ds(start + f, HARMONICS, stride=both + 1), :] = harmonic_rows(source[f].astype(jnp.float32))
        rows[pl.ds(start, count), :] = source[count].astype(jnp.float32)[0:count]
    for m in range(HARMONICS):
        out[m] = scratch[pl.ds(m * (both + 1), both), :].astype(jnp.bfloat16)
    out[HARMONICS] = rows[...].astype(jnp.bfloat16)


def arrange(core, mine, theirs):
    both = 2 * (mine.shape[0] - 1)
    return pl.pallas_call(
        arrange_kernel,
        out_shape=jax.ShapeDtypeStruct((HARMONICS + 1, both, 128), jnp.bfloat16),
        in_specs=[SMEM, VMEM, VMEM],
        out_specs=VMEM,
        scratch_shapes=[
            pltpu.VMEM((HARMONICS * (both + 1), 128), jnp.float32),
            pltpu.VMEM((both, 128), jnp.float32),
        ],
        name="arrange",
    )(core, mine, theirs)


def split(value):
    high = value.astype(jnp.bfloat16)
    return high, (value - high.astype(jnp.float32)).astype(jnp.bfloat16)


def dot(a, b):
    return jnp.dot(a, b, preferred_element_type=jnp.float32)


def project_kernel(harmonics, *refs):
    *pieces, high_out, low_out = refs
    ids = jnp.concatenate([ref[j, 0] for ref in pieces for j in range(ref.shape[0])], axis=0).astype(jnp.float32)
    bins = (ids[:, 0:1] * 32.0 + ids[:, 1:2]).astype(jnp.int32)
    onehot = (lax.broadcasted_iota(jnp.int32, (ids.shape[0], BINS), 1) == bins).astype(jnp.float32).astype(jnp.bfloat16)
    high, low = split(harmonics[...])
    high_out[...] = dot(onehot, high).astype(jnp.bfloat16)
    low_out[...] = dot(onehot, low).astype(jnp.bfloat16)


def project(harmonics, pieces):
    rows = sum(piece.shape[0] * piece.shape[2] for piece in pieces)
    shape = jax.ShapeDtypeStruct((rows, COEFS), jnp.bfloat16)
    spec = pl.BlockSpec((rows, COEFS), lambda i: (0, 0))
    return pl.pallas_call(
        project_kernel,
        grid=(1,),
        out_shape=(shape, shape),
        in_specs=[pl.BlockSpec((BINS, COEFS), lambda i: (0, 0))]
        + [pl.BlockSpec((p.shape[0], 1) + p.shape[2:], lambda i: (0, HARMONICS, 0, 0)) for p in pieces],
        out_specs=(spec, spec),
        compiler_params=pltpu.CompilerParams(vmem_limit_bytes=16 << 20),
        name="project",
    )(harmonics, *pieces)


def score_kernel(*refs, blocks, pieces, chained):
    frame_refs = refs[:blocks]
    piece_refs = refs[blocks : blocks + pieces]
    refs = refs[blocks + pieces :]
    table, high_ref, low_ref = refs[:3]
    before = refs[3] if chained else None
    out, cross, per_template, turned, scale, reference = refs[-6:]
    size = frame_refs[0].shape[1]
    count = blocks * size
    templates = high_ref.shape[0]
    tiles = templates // 128

    def correlate(m, _):
        plain = jnp.concatenate([ref[m] for ref in frame_refs], axis=0).astype(jnp.float32)
        quarter = jnp.concatenate([plain[:, HARMONICS:], -plain[:, :HARMONICS]], axis=1)
        rows = jnp.concatenate([plain, quarter], axis=0).astype(jnp.bfloat16)
        columns = jnp.concatenate([ref[j, m] for ref in piece_refs for j in range(ref.shape[0])], axis=0)
        result = lax.dot_general(
            rows, columns, (((1,), (1,)), ((), ())), preferred_element_type=jnp.float32
        )
        for s in range(2):
            for j in range(tiles):
                cross[j, pl.ds(s * HARMONICS + m, count, stride=STRIDE), :] = result[
                    s * count : (s + 1) * count, j * 128 : (j + 1) * 128
                ]
        return 0

    lax.fori_loop(0, HARMONICS, correlate, 0, unroll=8)
    lengths = jnp.concatenate([ref[HARMONICS] for ref in frame_refs], axis=0).astype(jnp.float32)
    scale[...] = LOG2E / (8.0 * jnp.sqrt(lengths))
    lane = lax.broadcasted_iota(jnp.int32, (ANGLES, 128), 1)
    turned[...] = jnp.zeros_like(turned)

    def sums(f, exact):
        factor = scale[pl.ds(f, 1), :]
        factor = jnp.concatenate([factor] * 2, axis=1)
        scores = []
        for h in range(tiles // 2):
            spectra = jnp.concatenate(
                [cross[2 * h + j, pl.ds(f * STRIDE, 128), :].astype(jnp.bfloat16) for j in range(2)], axis=1
            )
            scores.append(dot(table[...], spectra) * factor)
        if exact:
            top = functools.reduce(jnp.maximum, [jnp.max(s, axis=(0, 1), keepdims=True) for s in scores])
            scores = [s - top for s in scores]
            reference[pl.ds(f, 1), :] = jnp.broadcast_to(top, (1, 128))
        across = None
        for h, s in enumerate(scores):
            weights = jnp.exp2(s)
            per_template[pl.ds(f, 1), h * 256 : (h + 1) * 256] = jnp.sum(weights, axis=0, keepdims=True)
            folded = weights[:, :128] + weights[:, 128:]
            across = folded if across is None else across + folded
        turned[...] = jnp.where(lane == f, jnp.sum(across, axis=1, keepdims=True), turned[...])

    reference[...] = jnp.zeros_like(reference)
    lax.fori_loop(0, count, lambda f, _: (sums(f, False), 0)[1], 0, unroll=8)
    totals = jnp.sum(per_template[...], axis=1, keepdims=True)
    safe = jnp.logical_and(jnp.max(totals) < 1e30, jnp.min(totals) > 1e-20)

    @pl.when(jnp.logical_not(safe))
    def _():
        lax.fori_loop(0, count, lambda f, _: (sums(f, True), 0)[1], 0)

    weights = per_template[...]
    totals = jnp.sum(weights, axis=1, keepdims=True)
    high, low = split(weights)
    summary = jnp.concatenate(
        [
            dot(high, high_ref[...]) + (dot(high, low_ref[...]) + dot(low, high_ref[...])),
            turned[...].T[:count],
            jnp.where(lax.broadcasted_iota(jnp.int32, (count, 128), 1) == 0, totals, reference[...]),
        ],
        axis=1,
    )
    if chained:
        summary = merged([before[...], summary])
    out[...] = summary


def merged(summaries):
    references = [s[:, TOT + 1 : TOT + 2] for s in summaries]
    top = functools.reduce(jnp.maximum, references)
    total = None
    for s, r in zip(summaries, references):
        term = s * jnp.exp2(r - top)
        total = term if total is None else total + term
    column = lax.broadcasted_iota(jnp.int32, total.shape, 1)
    return jnp.where(column > TOT, top, total)


def score(frame_blocks, pieces, table, projection, before=None):
    count = sum(block.shape[1] for block in frame_blocks)
    templates = projection[0].shape[0]
    chained = before is not None
    operands = (*frame_blocks, *pieces, table, *projection) + ((before,) if chained else ())
    pairs = count * templates
    return pl.pallas_call(
        functools.partial(score_kernel, blocks=len(frame_blocks), pieces=len(pieces), chained=chained),
        out_shape=jax.ShapeDtypeStruct((count, WIDTH), jnp.float32),
        in_specs=[VMEM] * len(operands),
        out_specs=VMEM,
        scratch_shapes=[
            pltpu.VMEM((templates // 128, count * STRIDE, 128), jnp.float32),
            pltpu.VMEM((count, templates), jnp.float32),
            pltpu.VMEM((ANGLES, 128), jnp.float32),
            pltpu.VMEM((count, 128), jnp.float32),
            pltpu.VMEM((count, 128), jnp.float32),
        ],
        compiler_params=pltpu.CompilerParams(vmem_limit_bytes=28 << 20),
        cost_estimate=pl.CostEstimate(flops=pairs * 65536, bytes_accessed=8 << 20, transcendentals=pairs * ANGLES),
        name="score",
    )(*operands)


def gather_kernel(core, first, second, third, fourth, keep, send):
    whole = merged([first[...], second[...], third[...], fourth[...]])
    count = keep.shape[0]
    low, high = whole[:count], whole[count:]
    keep[...] = jnp.where(core[0] == 0, low, high)
    send[...] = jnp.where(core[0] == 0, high, low)


def gather(core, summaries):
    both = summaries[0].shape[0]
    half = jax.ShapeDtypeStruct((both // 2, WIDTH), jnp.float32)
    return pl.pallas_call(
        gather_kernel,
        out_shape=(half, half),
        in_specs=[SMEM] + [VMEM] * 4,
        out_specs=(VMEM, VMEM),
        name="gather",
    )(core, *summaries)


def finish_kernel(mine, theirs, coefficients, rotations):
    total = merged([mine[...], theirs[...]])
    inverse = 1.0 / total[:, TOT : TOT + 1]
    coefficients[...] = total[:, :ROT] * inverse
    rotations[...] = total[:, ROT:TOT] * inverse


def finish(mine, theirs):
    count = mine.shape[0]
    return pl.pallas_call(
        finish_kernel,
        out_shape=(
            jax.ShapeDtypeStruct((count, COEFS), jnp.float32),
            jax.ShapeDtypeStruct((count, ANGLES), jnp.float32),
        ),
        in_specs=[VMEM, VMEM],
        out_specs=(VMEM, VMEM),
        name="finish",
    )(mine, theirs)


def local(frames, lengths, templates, bin_ids, harmonics):
    core_index = lax.axis_index("frames") % 2
    core = core_index.reshape(1).astype(jnp.int32)
    table = rotation_table()
    raw, tmpl = prepare(lengths, bin_ids, frames, templates)
    raw_other = swap(raw)
    row = jnp.stack([tmpl, first_axis(tmpl, 1), first_axis(tmpl, -1), first_axis(tmpl, 2)])
    chip = arrange(core, raw, raw_other)
    ring1 = along_z(chip, 1)
    above = second_axis(row, 1)
    below = second_axis(row, -1)
    ring2 = along_z(ring1, 1)
    far1 = second_axis(above[:2], 1)
    far2 = second_axis(below[2:], -1)
    ring3 = along_z(ring2, 1)
    last = jnp.where(core_index == 0, chip, ring3)
    ring0 = move(last, lambda core: (0, 0, 0 if core == 0 else -1, 0))
    own = (row, above, below, far1, far2)
    other = tuple(swap(piece) for piece in own)
    own_projection = project(harmonics, own)
    other_projection = project(harmonics, other)

    half1 = score((ring1, ring2), own, table, own_projection)
    half2 = score((ring3, ring0), own, table, own_projection)
    done1 = score((ring1, ring2), other, table, other_projection, half1)
    done2 = score((ring3, ring0), other, table, other_projection, half2)
    size = ring1.shape[1]
    home1 = along_z(done1[:size], -1)
    home2 = along_z(done1[size:], -2)
    home3 = along_z(done2[:size], -3)
    home0 = move(done2[size:], lambda core: (0, 0, 0 if core == 0 else 4, 0))
    keep, send = gather(core, (home1, home2, home3, home0))
    return finish(keep, swap(send))


def solution(mesh):
    return jax.shard_map(
        local,
        mesh=mesh,
        in_specs=(
            P(AXES, None, None),
            P(AXES),
            P(AXES, None, None),
            P(AXES),
            P(),
        ),
        out_specs=(P(AXES, None), P(AXES, None)),
        check_vma=False,
    )
```

```python
import functools
import math

import jax
import jax.numpy as jnp
from jax import lax
from jax.experimental import pallas as pl
from jax.experimental.pallas import tpu as pltpu
from jax.sharding import PartitionSpec as P

RADII = 64
HARMONICS = 64
ANGLES = 128
COEFS = 512
BINS = 1024
WIDTH = 768
ROT = COEFS
TOT = COEFS + ANGLES
STRIDE = 129
LOG2E = math.log2(math.e)
AXES = ("frames", "tmpl")
VMEM = pl.BlockSpec(memory_space=pltpu.VMEM)
SMEM = pl.BlockSpec(memory_space=pltpu.SMEM)
CHIPS_X, CHIPS_Y, CHIPS_Z = 4, 4, 8


def device(x, y, z, core):
    return (((x * 2 + y // 2) * 2 + core) * 2 + y % 2) * CHIPS_Z + z


def move(value, step):
    pairs = []
    for x in range(CHIPS_X):
        for y in range(CHIPS_Y):
            for z in range(CHIPS_Z):
                for core in range(2):
                    dx, dy, dz, dc = step(core)
                    there = device((x + dx) % CHIPS_X, (y + dy) % CHIPS_Y, (z + dz) % CHIPS_Z, (core + dc) % 2)
                    pairs.append((device(x, y, z, core), there))
    return lax.ppermute(value, AXES, pairs)


def swap(value):
    return move(value, lambda core: (0, 0, 0, 1))


def along_z(value, steps):
    return move(value, lambda core: (0, 0, steps if core == 0 else -steps, 0))


def first_axis(value, steps):
    return move(value, lambda core: (steps, 0, 0, 0) if core == 0 else (0, steps, 0, 0))


def second_axis(value, steps):
    return move(value, lambda core: (0, steps, 0, 0) if core == 0 else (steps, 0, 0, 0))


def after(value, *others):
    return lax.optimization_barrier((value, others))[0]


def rotation_table():
    harmonic = lax.broadcasted_iota(jnp.int32, (HARMONICS, ANGLES), 0)
    angle_index = lax.broadcasted_iota(jnp.int32, (HARMONICS, ANGLES), 1)
    phases = (harmonic * angle_index % ANGLES).astype(jnp.float32) * (2.0 * math.pi / ANGLES)
    weight = jnp.where(harmonic == 0, 1.0, 2.0).astype(jnp.float32)
    table = jnp.concatenate([weight * jnp.cos(phases), -weight * jnp.sin(phases)], axis=0)
    return table.astype(jnp.bfloat16).T


def harmonic_rows(spectrum):
    turned = spectrum.T
    return jnp.concatenate([turned[:HARMONICS], turned[HARMONICS:]], axis=1)


def templates_kernel(bins, templates, tmpl, scratch, rows):
    size = templates.shape[0]
    for t in range(size):
        scratch[pl.ds(t, HARMONICS, stride=size + 1), :] = harmonic_rows(templates[t].astype(jnp.float32))
    for m in range(HARMONICS):
        tmpl[m] = scratch[pl.ds(m * (size + 1), size), :].astype(jnp.bfloat16)
    lane = lax.broadcasted_iota(jnp.int32, (1, 128), 1)
    for t in range(size):
        high, low = (bins[t] >> 5).astype(jnp.float32), (bins[t] & 31).astype(jnp.float32)
        rows[t : t + 1, :] = jnp.where(lane == 0, high, low)
    tmpl[HARMONICS] = rows[...].astype(jnp.bfloat16)


def prepare_templates(bins, templates):
    size = templates.shape[0]
    return pl.pallas_call(
        templates_kernel,
        out_shape=jax.ShapeDtypeStruct((HARMONICS + 1, size, 128), jnp.bfloat16),
        in_specs=[SMEM, VMEM],
        out_specs=VMEM,
        scratch_shapes=[
            pltpu.VMEM((HARMONICS * (size + 1), 128), jnp.float32),
            pltpu.VMEM((size, 128), jnp.float32),
        ],
        name="prepare_templates",
    )(bins, templates)


def frames_kernel(lengths, frames, raw, rows):
    count = frames.shape[0]
    radius = lax.broadcasted_iota(jnp.int32, (RADII, 2 * HARMONICS), 0)
    rows[...] = jnp.zeros_like(rows)
    for f in range(count):
        raw[f] = jnp.where(radius < lengths[f], frames[f].astype(jnp.float32), 0.0).astype(jnp.bfloat16)
        rows[f : f + 1, :] = jnp.full((1, 128), lengths[f].astype(jnp.float32))
    raw[count] = rows[...].astype(jnp.bfloat16)


def prepare_frames(lengths, frames):
    return pl.pallas_call(
        frames_kernel,
        out_shape=jax.ShapeDtypeStruct((frames.shape[0] + 1, RADII, 128), jnp.bfloat16),
        in_specs=[SMEM, VMEM],
        out_specs=VMEM,
        scratch_shapes=[pltpu.VMEM((RADII, 128), jnp.float32)],
        name="prepare_frames",
    )(lengths, frames)


def arrange_kernel(core, mine, theirs, out, scratch, rows):
    count = mine.shape[0] - 1
    both = 2 * count
    here = core[0] * count
    there = count - here
    for source, start in ((mine, here), (theirs, there)):
        for f in range(count):
            scratch[pl.ds(start + f, HARMONICS, stride=both + 1), :] = harmonic_rows(source[f].astype(jnp.float32))
        rows[pl.ds(start, count), :] = source[count].astype(jnp.float32)[0:count]
    for m in range(HARMONICS):
        out[m] = scratch[pl.ds(m * (both + 1), both), :].astype(jnp.bfloat16)
    out[HARMONICS] = rows[...].astype(jnp.bfloat16)


def arrange(core, mine, theirs):
    both = 2 * (mine.shape[0] - 1)
    return pl.pallas_call(
        arrange_kernel,
        out_shape=jax.ShapeDtypeStruct((HARMONICS + 1, both, 128), jnp.bfloat16),
        in_specs=[SMEM, VMEM, VMEM],
        out_specs=VMEM,
        scratch_shapes=[
            pltpu.VMEM((HARMONICS * (both + 1), 128), jnp.float32),
            pltpu.VMEM((both, 128), jnp.float32),
        ],
        name="arrange",
    )(core, mine, theirs)


def split(value):
    high = value.astype(jnp.bfloat16)
    return high, (value - high.astype(jnp.float32)).astype(jnp.bfloat16)


def dot(a, b):
    return jnp.dot(a, b, preferred_element_type=jnp.float32)


def project_kernel(harmonics, *refs):
    *pieces, high_out, low_out = refs
    ids = jnp.concatenate([ref[j, 0] for ref in pieces for j in range(ref.shape[0])], axis=0).astype(jnp.float32)
    bins = (ids[:, 0:1] * 32.0 + ids[:, 1:2]).astype(jnp.int32)
    onehot = (lax.broadcasted_iota(jnp.int32, (ids.shape[0], BINS), 1) == bins).astype(jnp.float32).astype(jnp.bfloat16)
    high, low = split(harmonics[...])
    high_out[...] = dot(onehot, high).astype(jnp.bfloat16)
    low_out[...] = dot(onehot, low).astype(jnp.bfloat16)


def project(harmonics, pieces):
    rows = sum(piece.shape[0] * piece.shape[2] for piece in pieces)
    shape = jax.ShapeDtypeStruct((rows, COEFS), jnp.bfloat16)
    spec = pl.BlockSpec((rows, COEFS), lambda i: (0, 0))
    return pl.pallas_call(
        project_kernel,
        grid=(1,),
        out_shape=(shape, shape),
        in_specs=[pl.BlockSpec((BINS, COEFS), lambda i: (0, 0))]
        + [pl.BlockSpec((p.shape[0], 1) + p.shape[2:], lambda i: (0, HARMONICS, 0, 0)) for p in pieces],
        out_specs=(spec, spec),
        compiler_params=pltpu.CompilerParams(vmem_limit_bytes=16 << 20),
        name="project",
    )(harmonics, *pieces)


def score_kernel(core, *refs, blocks, pieces, chained, last):
    frame_refs = refs[:blocks]
    piece_refs = refs[blocks : blocks + pieces]
    refs = refs[blocks + pieces :]
    table, high_ref, low_ref = refs[:3]
    before = refs[3 : 3 + blocks] if chained else None
    outs = refs[3 + blocks if chained else 3 : -5]
    cross, per_template, turned, scale, reference = refs[-5:]
    size = frame_refs[0].shape[1]
    count = blocks * size
    templates = high_ref.shape[0]
    tiles = templates // 128

    def correlate(m, _):
        plain = jnp.concatenate([ref[m] for ref in frame_refs], axis=0).astype(jnp.float32)
        quarter = jnp.concatenate([plain[:, HARMONICS:], -plain[:, :HARMONICS]], axis=1)
        rows = jnp.concatenate([plain, quarter], axis=0).astype(jnp.bfloat16)
        columns = jnp.concatenate([ref[j, m] for ref in piece_refs for j in range(ref.shape[0])], axis=0)
        result = lax.dot_general(
            rows, columns, (((1,), (1,)), ((), ())), preferred_element_type=jnp.float32
        )
        for s in range(2):
            for j in range(tiles):
                cross[j, pl.ds(s * HARMONICS + m, count, stride=STRIDE), :] = result[
                    s * count : (s + 1) * count, j * 128 : (j + 1) * 128
                ]
        return 0

    lax.fori_loop(0, HARMONICS, correlate, 0, unroll=64)
    lengths = jnp.concatenate([ref[HARMONICS] for ref in frame_refs], axis=0).astype(jnp.float32)
    scale[...] = LOG2E / (8.0 * jnp.sqrt(lengths))
    lane = lax.broadcasted_iota(jnp.int32, (ANGLES, 128), 1)
    turned[...] = jnp.zeros_like(turned)

    def sums(f, exact):
        factor = scale[pl.ds(f, 1), :]
        factor = jnp.concatenate([factor] * 2, axis=1)
        scores = []
        for h in range(tiles // 2):
            spectra = jnp.concatenate(
                [cross[2 * h + j, pl.ds(f * STRIDE, 128), :].astype(jnp.bfloat16) for j in range(2)], axis=1
            )
            scores.append(dot(table[...], spectra) * factor)
        if exact:
            top = functools.reduce(jnp.maximum, [jnp.max(s, axis=(0, 1), keepdims=True) for s in scores])
            scores = [s - top for s in scores]
            reference[pl.ds(f, 1), :] = jnp.broadcast_to(top, (1, 128))
        across = None
        for h, s in enumerate(scores):
            weights = jnp.exp2(s)
            per_template[pl.ds(f, 1), h * 256 : (h + 1) * 256] = jnp.sum(weights, axis=0, keepdims=True)
            folded = weights[:, :128] + weights[:, 128:]
            across = folded if across is None else across + folded
        turned[...] = jnp.where(lane == f, jnp.sum(across, axis=1, keepdims=True), turned[...])

    reference[...] = jnp.zeros_like(reference)
    lax.fori_loop(0, count, lambda f, _: (sums(f, False), 0)[1], 0, unroll=40)
    totals = jnp.sum(per_template[...], axis=1, keepdims=True)
    safe = jnp.logical_and(jnp.max(totals) < 1e30, jnp.min(totals) > 1e-20)

    @pl.when(jnp.logical_not(safe))
    def _():
        lax.fori_loop(0, count, lambda f, _: (sums(f, True), 0)[1], 0)

    weights = per_template[...]
    totals = jnp.sum(weights, axis=1, keepdims=True)
    high, low = split(weights)
    summary = jnp.concatenate(
        [
            dot(high, high_ref[...]) + (dot(high, low_ref[...]) + dot(low, high_ref[...])),
            turned[...].T[:count],
            jnp.where(lax.broadcasted_iota(jnp.int32, (count, 128), 1) == 0, totals, reference[...]),
        ],
        axis=1,
    )
    if chained:
        summary = merged([jnp.concatenate([ref[...] for ref in before], axis=0), summary])
    if last:
        half = size // 2
        low, high = summary[:half], summary[half:]
        outs[0][...] = jnp.where(core[0] == 0, low, high)
        outs[1][...] = jnp.where(core[0] == 0, high, low)
    else:
        for block, out in enumerate(outs):
            out[...] = summary[block * size : (block + 1) * size]


def merged(summaries):
    references = [s[:, TOT + 1 : TOT + 2] for s in summaries]
    top = functools.reduce(jnp.maximum, references)
    total = None
    for s, r in zip(summaries, references):
        term = s * jnp.exp2(r - top)
        total = term if total is None else total + term
    column = lax.broadcasted_iota(jnp.int32, total.shape, 1)
    return jnp.where(column > TOT, top, total)


def score(core, frame_blocks, pieces, table, projection, before=None, last=False):
    size = frame_blocks[0].shape[1]
    blocks = len(frame_blocks)
    count = blocks * size
    templates = projection[0].shape[0]
    chained = before is not None
    operands = (*frame_blocks, *pieces, table, *projection) + (tuple(before) if chained else ())
    pairs = count * templates
    rows = size // 2 if last else size
    outs = 2 if last else blocks
    return pl.pallas_call(
        functools.partial(score_kernel, blocks=blocks, pieces=len(pieces), chained=chained, last=last),
        out_shape=(jax.ShapeDtypeStruct((rows, WIDTH), jnp.float32),) * outs,
        in_specs=[SMEM] + [VMEM] * len(operands),
        out_specs=(VMEM,) * outs,
        scratch_shapes=[
            pltpu.VMEM((templates // 128, count * STRIDE, 128), jnp.float32),
            pltpu.VMEM((count, templates), jnp.float32),
            pltpu.VMEM((ANGLES, 128), jnp.float32),
            pltpu.VMEM((count, 128), jnp.float32),
            pltpu.VMEM((count, 128), jnp.float32),
        ],
        compiler_params=pltpu.CompilerParams(vmem_limit_bytes=28 << 20),
        cost_estimate=pl.CostEstimate(
            flops=pairs * 65536 * 6, bytes_accessed=8 << 20, transcendentals=pairs * ANGLES
        ),
        name="score",
    )(core, *operands)


def gather_kernel(core, first, second, third, fourth, keep, send):
    whole = merged([first[...], second[...], third[...], fourth[...]])
    count = keep.shape[0]
    low, high = whole[:count], whole[count:]
    keep[...] = jnp.where(core[0] == 0, low, high)
    send[...] = jnp.where(core[0] == 0, high, low)


def gather(core, summaries):
    both = summaries[0].shape[0]
    half = jax.ShapeDtypeStruct((both // 2, WIDTH), jnp.float32)
    return pl.pallas_call(
        gather_kernel,
        out_shape=(half, half),
        in_specs=[SMEM] + [VMEM] * 4,
        out_specs=(VMEM, VMEM),
        name="gather",
    )(core, *summaries)


def finish_kernel(*refs):
    *summaries, coefficients, rotations = refs
    total = merged([ref[...] for ref in summaries])
    inverse = 1.0 / total[:, TOT : TOT + 1]
    coefficients[...] = total[:, :ROT] * inverse
    rotations[...] = total[:, ROT:TOT] * inverse


def finish(*summaries):
    count = summaries[0].shape[0]
    return pl.pallas_call(
        finish_kernel,
        out_shape=(
            jax.ShapeDtypeStruct((count, COEFS), jnp.float32),
            jax.ShapeDtypeStruct((count, ANGLES), jnp.float32),
        ),
        in_specs=[VMEM] * len(summaries),
        out_specs=(VMEM, VMEM),
        name="finish",
    )(*summaries)


def local(frames, lengths, templates, bin_ids, harmonics):
    core = (lax.axis_index("frames") % 2).reshape(1).astype(jnp.int32)
    table = rotation_table()
    tmpl = prepare_templates(bin_ids, templates)
    ahead = first_axis(tmpl, 1)
    behind = first_axis(tmpl, -1)
    opposite = first_axis(tmpl, 2)
    raw = prepare_frames(lengths, frames)
    chip = arrange(core, raw, swap(raw))
    ahead = after(ahead, chip)
    ring1 = along_z(chip, 1)
    row1 = jnp.stack([tmpl, ahead])
    above1 = second_axis(row1, 1)
    below1 = second_axis(row1, -1)
    row2 = jnp.stack([behind, opposite])
    above2 = second_axis(row2, 1)
    below2 = second_axis(row2, -1)
    far1 = second_axis(above1, 1)
    far2 = second_axis(below2, -1)
    ring2 = along_z(ring1, 1)
    own = (row1, row2, above1, below1, above2, below2, far1, far2)
    own_projection = project(harmonics, own)
    stay, first, second = score(core, (chip, ring1, ring2), own, table, own_projection)
    ring3 = along_z(ring2, 1)
    other = (
        swap(jnp.concatenate([row1, row2])),
        swap(jnp.concatenate([above1, below1])),
        swap(jnp.concatenate([above2, below2])),
        swap(jnp.concatenate([far1, far2])),
    )
    other = after(other, second)
    other_projection = project(harmonics, other)
    first, second = score(core, (ring1, ring2), other, table, other_projection, (first, second))
    home1 = along_z(first, -1)
    home2 = along_z(second, -2)
    ring4 = along_z(ring3, 1)
    ring3, ring4 = after((ring3, ring4), second)
    third, fourth = score(core, (ring3, ring4), own, table, own_projection)
    home4 = along_z(fourth, -4)
    here, there = score(core, (ring3,), other, table, other_projection, (third,), last=True)
    keep, send = gather(core, (home1, home2, home4, stay))
    home3 = along_z(here, -3)
    across3 = move(there, lambda core: (0, 0, -3 if core == 0 else 3, 1))
    return finish(keep, swap(send), home3, across3)


def solution(mesh):
    return jax.shard_map(
        local,
        mesh=mesh,
        in_specs=(
            P(AXES, None, None),
            P(AXES),
            P(AXES, None, None),
            P(AXES),
            P(),
        ),
        out_specs=(P(AXES, None), P(AXES, None)),
        check_vma=False,
    )
```

```python
import functools
import math

import jax
import jax.numpy as jnp
from jax import lax
from jax.experimental import pallas as pl
from jax.experimental.pallas import tpu as pltpu
from jax.sharding import PartitionSpec as P

RADII = 64
HARMONICS = 64
ANGLES = 128
COEFS = 512
BINS = 1024
WIDTH = 768
ROT = COEFS
TOT = COEFS + ANGLES
STRIDE = 129
LOG2E = math.log2(math.e)
AXES = ("frames", "tmpl")
VMEM = pl.BlockSpec(memory_space=pltpu.VMEM)
SMEM = pl.BlockSpec(memory_space=pltpu.SMEM)
CHIPS_X, CHIPS_Y, CHIPS_Z = 4, 4, 8


def device(x, y, z, core):
    return (((x * 2 + y // 2) * 2 + core) * 2 + y % 2) * CHIPS_Z + z


def move(value, step):
    pairs = []
    for x in range(CHIPS_X):
        for y in range(CHIPS_Y):
            for z in range(CHIPS_Z):
                for core in range(2):
                    dx, dy, dz, dc = step(core)
                    there = device((x + dx) % CHIPS_X, (y + dy) % CHIPS_Y, (z + dz) % CHIPS_Z, (core + dc) % 2)
                    pairs.append((device(x, y, z, core), there))
    return lax.ppermute(value, AXES, pairs)


def swap(value):
    return move(value, lambda core: (0, 0, 0, 1))


def along_z(value, steps):
    return move(value, lambda core: (0, 0, steps if core == 0 else -steps, 0))


def first_axis(value, steps):
    return move(value, lambda core: (steps, 0, 0, 0) if core == 0 else (0, steps, 0, 0))


def second_axis(value, steps):
    return move(value, lambda core: (0, steps, 0, 0) if core == 0 else (steps, 0, 0, 0))


def after(value, *others):
    return lax.optimization_barrier((value, others))[0]


def rotation_table():
    harmonic = lax.broadcasted_iota(jnp.int32, (HARMONICS, ANGLES), 0)
    angle_index = lax.broadcasted_iota(jnp.int32, (HARMONICS, ANGLES), 1)
    phases = (harmonic * angle_index % ANGLES).astype(jnp.float32) * (2.0 * math.pi / ANGLES)
    weight = jnp.where(harmonic == 0, 1.0, 2.0).astype(jnp.float32)
    table = jnp.concatenate([weight * jnp.cos(phases), -weight * jnp.sin(phases)], axis=0)
    return table.astype(jnp.bfloat16).T


def harmonic_rows(spectrum):
    turned = spectrum.T
    return jnp.concatenate([turned[:HARMONICS], turned[HARMONICS:]], axis=1)


def templates_kernel(bins, templates, tmpl, scratch, rows):
    size = templates.shape[0]
    for t in range(size):
        scratch[pl.ds(t, HARMONICS, stride=size + 1), :] = harmonic_rows(templates[t].astype(jnp.float32))
    for m in range(HARMONICS):
        tmpl[m] = scratch[pl.ds(m * (size + 1), size), :].astype(jnp.bfloat16)
    lane = lax.broadcasted_iota(jnp.int32, (1, 128), 1)
    for t in range(size):
        high, low = (bins[t] >> 5).astype(jnp.float32), (bins[t] & 31).astype(jnp.float32)
        rows[t : t + 1, :] = jnp.where(lane == 0, high, low)
    tmpl[HARMONICS] = rows[...].astype(jnp.bfloat16)


def prepare_templates(bins, templates):
    size = templates.shape[0]
    return pl.pallas_call(
        templates_kernel,
        out_shape=jax.ShapeDtypeStruct((HARMONICS + 1, size, 128), jnp.bfloat16),
        in_specs=[SMEM, VMEM],
        out_specs=VMEM,
        scratch_shapes=[
            pltpu.VMEM((HARMONICS * (size + 1), 128), jnp.float32),
            pltpu.VMEM((size, 128), jnp.float32),
        ],
        name="prepare_templates",
    )(bins, templates)


def frames_kernel(lengths, frames, raw, rows):
    count = frames.shape[0]
    radius = lax.broadcasted_iota(jnp.int32, (RADII, 2 * HARMONICS), 0)
    rows[...] = jnp.zeros_like(rows)
    for f in range(count):
        raw[f] = jnp.where(radius < lengths[f], frames[f].astype(jnp.float32), 0.0).astype(jnp.bfloat16)
        rows[f : f + 1, :] = jnp.full((1, 128), lengths[f].astype(jnp.float32))
    raw[count] = rows[...].astype(jnp.bfloat16)


def prepare_frames(lengths, frames):
    return pl.pallas_call(
        frames_kernel,
        out_shape=jax.ShapeDtypeStruct((frames.shape[0] + 1, RADII, 128), jnp.bfloat16),
        in_specs=[SMEM, VMEM],
        out_specs=VMEM,
        scratch_shapes=[pltpu.VMEM((RADII, 128), jnp.float32)],
        name="prepare_frames",
    )(lengths, frames)


def arrange_kernel(core, mine, theirs, out, scratch, rows):
    count = mine.shape[0] - 1
    both = 2 * count
    here = core[0] * count
    there = count - here
    for source, start in ((mine, here), (theirs, there)):
        for f in range(count):
            scratch[pl.ds(start + f, HARMONICS, stride=both + 1), :] = harmonic_rows(source[f].astype(jnp.float32))
        rows[pl.ds(start, count), :] = source[count].astype(jnp.float32)[0:count]
    for m in range(HARMONICS):
        out[m] = scratch[pl.ds(m * (both + 1), both), :].astype(jnp.bfloat16)
    out[HARMONICS] = rows[...].astype(jnp.bfloat16)


def arrange(core, mine, theirs):
    both = 2 * (mine.shape[0] - 1)
    return pl.pallas_call(
        arrange_kernel,
        out_shape=jax.ShapeDtypeStruct((HARMONICS + 1, both, 128), jnp.bfloat16),
        in_specs=[SMEM, VMEM, VMEM],
        out_specs=VMEM,
        scratch_shapes=[
            pltpu.VMEM((HARMONICS * (both + 1), 128), jnp.float32),
            pltpu.VMEM((both, 128), jnp.float32),
        ],
        name="arrange",
    )(core, mine, theirs)


def split(value):
    high = value.astype(jnp.bfloat16)
    return high, (value - high.astype(jnp.float32)).astype(jnp.bfloat16)


def dot(a, b):
    return jnp.dot(a, b, preferred_element_type=jnp.float32)


def project_kernel(harmonics, *refs):
    *pieces, high_out, low_out = refs
    ids = jnp.concatenate([ref[j, 0] for ref in pieces for j in range(ref.shape[0])], axis=0).astype(jnp.float32)
    bins = (ids[:, 0:1] * 32.0 + ids[:, 1:2]).astype(jnp.int32)
    onehot = (lax.broadcasted_iota(jnp.int32, (ids.shape[0], BINS), 1) == bins).astype(jnp.float32).astype(jnp.bfloat16)
    high, low = split(harmonics[...])
    high_out[...] = dot(onehot, high).astype(jnp.bfloat16)
    low_out[...] = dot(onehot, low).astype(jnp.bfloat16)


def project(harmonics, pieces):
    rows = sum(piece.shape[0] * piece.shape[2] for piece in pieces)
    shape = jax.ShapeDtypeStruct((rows, COEFS), jnp.bfloat16)
    spec = pl.BlockSpec((rows, COEFS), lambda i: (0, 0))
    return pl.pallas_call(
        project_kernel,
        grid=(1,),
        out_shape=(shape, shape),
        in_specs=[pl.BlockSpec((BINS, COEFS), lambda i: (0, 0))]
        + [pl.BlockSpec((p.shape[0], 1) + p.shape[2:], lambda i: (0, HARMONICS, 0, 0)) for p in pieces],
        out_specs=(spec, spec),
        compiler_params=pltpu.CompilerParams(vmem_limit_bytes=16 << 20),
        name="project",
    )(harmonics, *pieces)


def score_kernel(core, *refs, blocks, pieces, halves, chained, cut):
    frame_refs = refs[:blocks]
    piece_refs = refs[blocks : blocks + pieces]
    table = refs[blocks + pieces]
    refs = refs[blocks + pieces + 1 :]
    projections = refs[: 2 * halves]
    refs = refs[2 * halves :]
    before = refs[:chained]
    outs = refs[chained:-5]
    cross, per_template, turned, scale, reference = refs[-5:]
    size = frame_refs[0].shape[1]
    count = blocks * size
    tiles = 2 * halves

    def correlate(m, _):
        plain = jnp.concatenate([ref[m] for ref in frame_refs], axis=0).astype(jnp.float32)
        quarter = jnp.concatenate([plain[:, HARMONICS:], -plain[:, :HARMONICS]], axis=1)
        rows = jnp.concatenate([plain, quarter], axis=0).astype(jnp.bfloat16)
        columns = jnp.concatenate([ref[j, m] for ref in piece_refs for j in range(ref.shape[0])], axis=0)
        result = lax.dot_general(
            rows, columns, (((1,), (1,)), ((), ())), preferred_element_type=jnp.float32
        )
        for s in range(2):
            for j in range(tiles):
                cross[j, pl.ds(s * HARMONICS + m, count, stride=STRIDE), :] = result[
                    s * count : (s + 1) * count, j * 128 : (j + 1) * 128
                ]
        return 0

    lax.fori_loop(0, HARMONICS, correlate, 0, unroll=64)
    lengths = jnp.concatenate([ref[HARMONICS] for ref in frame_refs], axis=0).astype(jnp.float32)
    scale[...] = LOG2E / (8.0 * jnp.sqrt(lengths))
    lane = lax.broadcasted_iota(jnp.int32, (ANGLES, 128), 1)
    turned[...] = jnp.zeros_like(turned)

    def sums(f, exact):
        factor = scale[pl.ds(f, 1), :]
        factor = jnp.concatenate([factor] * 2, axis=1)

        def scored(h):
            spectra = jnp.concatenate(
                [cross[2 * h + j, pl.ds(f * STRIDE, 128), :].astype(jnp.bfloat16) for j in range(2)], axis=1
            )
            return dot(table[...], spectra) * factor

        if exact:
            tops = [jnp.max(scored(h), axis=(0, 1), keepdims=True) for h in range(halves)]
            top = functools.reduce(jnp.maximum, tops)
            reference[pl.ds(f, 1), :] = jnp.broadcast_to(top, (1, 128))
        across = None
        for h in range(halves):
            weights = jnp.exp2(scored(h) - top if exact else scored(h))
            per_template[pl.ds(f, 1), h * 256 : (h + 1) * 256] = jnp.sum(weights, axis=0, keepdims=True)
            folded = weights[:, :128] + weights[:, 128:]
            across = folded if across is None else across + folded
        turned[...] = jnp.where(lane == f, jnp.sum(across, axis=1, keepdims=True), turned[...])

    reference[...] = jnp.zeros_like(reference)
    for f in range(count):
        sums(f, False)
    totals = jnp.sum(per_template[...], axis=1, keepdims=True)
    safe = jnp.logical_and(jnp.max(totals) < 1e30, jnp.min(totals) > 1e-20)

    @pl.when(jnp.logical_not(safe))
    def _():
        lax.fori_loop(0, count, lambda f, _: (sums(f, True), 0)[1], 0)

    weights = per_template[...]
    totals = jnp.sum(weights, axis=1, keepdims=True)
    coefficients = None
    for h in range(halves):
        high, low = split(weights[:, h * 256 : (h + 1) * 256])
        high_ref, low_ref = projections[2 * h : 2 * h + 2]
        part = dot(high, high_ref[...]) + (dot(high, low_ref[...]) + dot(low, high_ref[...]))
        coefficients = part if coefficients is None else coefficients + part
    summary = jnp.concatenate(
        [
            coefficients,
            turned[...].T[:count],
            jnp.where(lax.broadcasted_iota(jnp.int32, (count, 128), 1) == 0, totals, reference[...]),
        ],
        axis=1,
    )
    if chained:
        groups = [before[i : i + blocks] for i in range(0, chained, blocks)]
        summary = merged([jnp.concatenate([ref[...] for ref in group], axis=0) for group in groups] + [summary])
    if cut:
        half = size // 2
        low, high = summary[:half], summary[half:]
        outs[0][...] = jnp.where(core[0] == 0, low, high)
        outs[1][...] = jnp.where(core[0] == 0, high, low)
    else:
        for block, out in enumerate(outs):
            out[...] = summary[block * size : (block + 1) * size]


def merged(summaries):
    references = [s[:, TOT + 1 : TOT + 2] for s in summaries]
    top = functools.reduce(jnp.maximum, references)
    total = None
    for s, r in zip(summaries, references):
        term = s * jnp.exp2(r - top)
        total = term if total is None else total + term
    column = lax.broadcasted_iota(jnp.int32, total.shape, 1)
    return jnp.where(column > TOT, top, total)


def score(core, frame_blocks, pieces, table, projections, before=(), cut=False):
    blocks, halves, size = len(frame_blocks), len(projections), frame_blocks[0].shape[1]
    count, templates = blocks * size, halves * 256
    operands = (*frame_blocks, *pieces, table, *sum(projections, ()), *before)
    pairs = count * templates
    out = jax.ShapeDtypeStruct((size // 2 if cut else size, WIDTH), jnp.float32)
    outs = 2 if cut else blocks
    return pl.pallas_call(
        functools.partial(
            score_kernel, blocks=blocks, pieces=len(pieces), halves=halves, chained=len(before), cut=cut
        ),
        out_shape=(out,) * outs,
        in_specs=[SMEM] + [VMEM] * len(operands),
        out_specs=(VMEM,) * outs,
        scratch_shapes=[
            pltpu.VMEM((templates // 128, count * STRIDE, 128), jnp.float32),
            pltpu.VMEM((count, templates), jnp.float32),
            pltpu.VMEM((ANGLES, 128), jnp.float32),
            pltpu.VMEM((count, 128), jnp.float32),
            pltpu.VMEM((count, 128), jnp.float32),
        ],
        compiler_params=pltpu.CompilerParams(vmem_limit_bytes=28 << 20),
        cost_estimate=pl.CostEstimate(
            flops=pairs * 65536 * 12, bytes_accessed=8 << 20, transcendentals=pairs * ANGLES
        ),
        name="score",
    )(core, *operands)


def finish_kernel(*refs):
    *summaries, coefficients, rotations = refs
    total = merged([ref[...] for ref in summaries])
    inverse = 1.0 / total[:, TOT : TOT + 1]
    coefficients[...] = total[:, :ROT] * inverse
    rotations[...] = total[:, ROT:TOT] * inverse


def finish(*summaries):
    count = summaries[0].shape[0]
    return pl.pallas_call(
        finish_kernel,
        out_shape=(
            jax.ShapeDtypeStruct((count, COEFS), jnp.float32),
            jax.ShapeDtypeStruct((count, ANGLES), jnp.float32),
        ),
        in_specs=[VMEM] * len(summaries),
        out_specs=(VMEM, VMEM),
        name="finish",
    )(*summaries)


def local(frames, lengths, templates, bin_ids, harmonics):
    core = (lax.axis_index("frames") % 2).reshape(1).astype(jnp.int32)
    table = rotation_table()
    raw = prepare_frames(lengths, frames)
    tmpl = prepare_templates(bin_ids, after(templates, raw))
    ahead = first_axis(tmpl, 1)
    behind = first_axis(tmpl, -1)
    opposite = first_axis(tmpl, 2)
    chip = arrange(core, raw, swap(raw))
    ahead, behind, opposite = after((ahead, behind, opposite), chip)
    ring1 = along_z(chip, 1)
    row1 = jnp.stack([tmpl, ahead])
    above1 = second_axis(row1, 1)
    below1 = second_axis(row1, -1)
    row2 = jnp.stack([behind, opposite])
    above2 = second_axis(row2, 1)
    below2 = second_axis(row2, -1)
    above1, below2 = after((above1, below2), ring1)
    far1 = second_axis(above1, 1)
    far2 = second_axis(below2, -1)
    ring2 = along_z(ring1, 1)
    ring3 = along_z(ring2, 1)
    own = (row1, row2, above1, below1, above2, below2, far1, far2)
    own_projection = project(harmonics, own)
    near = score(core, (ring1, ring2), own, table, (own_projection,))
    other = (
        swap(jnp.concatenate([row1, row2])),
        swap(jnp.concatenate([above1, below1])),
        swap(jnp.concatenate([above2, below2])),
        swap(jnp.concatenate([far1, far2])),
    )
    other = after(other, near[0])
    other_projection = project(harmonics, other)
    first, second = score(core, (ring1, ring2), other, table, (other_projection,), near)
    home1 = along_z(first, -1)
    home2 = along_z(second, -2)
    ring4 = along_z(after(ring3, near[0]), 1)
    ring3 = after(ring3, second)
    (third,) = score(core, (ring3,), own + other, table, (own_projection, other_projection))
    home3 = along_z(third, -3)
    ring4 = after(ring4, third)
    fourth = score(core, (ring4,), own, table, (own_projection,), cut=True)
    home4 = go_home(*fourth, 4)
    chip = after(chip, fourth[0])
    keep, send = score(core, (chip,), own, table, (own_projection,), (home1, home2, home3), cut=True)
    send = after(send, home4)
    return finish(keep, swap(send), *home4)


def go_home(here, there, steps):
    return along_z(here, -steps), move(there, lambda core: (0, 0, -steps if core == 0 else steps, 1))


def solution(mesh):
    return jax.shard_map(
        local,
        mesh=mesh,
        in_specs=(
            P(AXES, None, None),
            P(AXES),
            P(AXES, None, None),
            P(AXES),
            P(),
        ),
        out_specs=(P(AXES, None), P(AXES, None)),
        check_vma=False,
    )
```

```python
import functools
import math

import jax
import jax.numpy as jnp
from jax import lax
from jax.experimental import pallas as pl
from jax.experimental.pallas import tpu as pltpu
from jax.sharding import PartitionSpec as P

RADII = 64
HARMONICS = 64
ANGLES = 128
COEFS = 512
BINS = 1024
WIDTH = 768
ROT = COEFS
TOT = COEFS + ANGLES
STRIDE = 129
LOG2E = math.log2(math.e)
AXES = ("frames", "tmpl")
VMEM = pl.BlockSpec(memory_space=pltpu.VMEM)
SMEM = pl.BlockSpec(memory_space=pltpu.SMEM)
CHIPS_X, CHIPS_Y, CHIPS_Z = 4, 4, 8


def device(x, y, z, core):
    return (((x * 2 + y // 2) * 2 + core) * 2 + y % 2) * CHIPS_Z + z


def move(value, step):
    pairs = []
    for x in range(CHIPS_X):
        for y in range(CHIPS_Y):
            for z in range(CHIPS_Z):
                for core in range(2):
                    dx, dy, dz, dc = step(core)
                    there = device((x + dx) % CHIPS_X, (y + dy) % CHIPS_Y, (z + dz) % CHIPS_Z, (core + dc) % 2)
                    pairs.append((device(x, y, z, core), there))
    return lax.ppermute(value, AXES, pairs)


def swap(value):
    return move(value, lambda core: (0, 0, 0, 1))


def along_z(value, steps):
    return move(value, lambda core: (0, 0, steps if core == 0 else -steps, 0))


def first_axis(value, steps):
    return move(value, lambda core: (steps, 0, 0, 0) if core == 0 else (0, steps, 0, 0))


def second_axis(value, steps):
    return move(value, lambda core: (0, steps, 0, 0) if core == 0 else (steps, 0, 0, 0))


def after(value, *others):
    return lax.optimization_barrier((value, others))[0]


def rotation_table():
    harmonic = lax.broadcasted_iota(jnp.int32, (HARMONICS, ANGLES), 0)
    angle_index = lax.broadcasted_iota(jnp.int32, (HARMONICS, ANGLES), 1)
    phases = (harmonic * angle_index % ANGLES).astype(jnp.float32) * (2.0 * math.pi / ANGLES)
    weight = jnp.where(harmonic == 0, 1.0, 2.0).astype(jnp.float32)
    table = jnp.concatenate([weight * jnp.cos(phases), -weight * jnp.sin(phases)], axis=0)
    return table.astype(jnp.bfloat16).T


def harmonic_rows(spectrum):
    turned = spectrum.T
    return jnp.concatenate([turned[:HARMONICS], turned[HARMONICS:]], axis=1)


def templates_kernel(bins, templates, tmpl, scratch, rows):
    size = templates.shape[0]
    for t in range(size):
        scratch[pl.ds(t, HARMONICS, stride=size + 1), :] = harmonic_rows(templates[t].astype(jnp.float32))
    for m in range(HARMONICS):
        tmpl[m] = scratch[pl.ds(m * (size + 1), size), :].astype(jnp.bfloat16)
    lane = lax.broadcasted_iota(jnp.int32, (1, 128), 1)
    for t in range(size):
        high, low = (bins[t] >> 5).astype(jnp.float32), (bins[t] & 31).astype(jnp.float32)
        rows[t : t + 1, :] = jnp.where(lane == 0, high, low)
    tmpl[HARMONICS] = rows[...].astype(jnp.bfloat16)


def prepare_templates(bins, templates):
    size = templates.shape[0]
    return pl.pallas_call(
        templates_kernel,
        out_shape=jax.ShapeDtypeStruct((HARMONICS + 1, size, 128), jnp.bfloat16),
        in_specs=[SMEM, VMEM],
        out_specs=VMEM,
        scratch_shapes=[
            pltpu.VMEM((HARMONICS * (size + 1), 128), jnp.float32),
            pltpu.VMEM((size, 128), jnp.float32),
        ],
        name="prepare_templates",
    )(bins, templates)


def frames_kernel(lengths, frames, raw, rows):
    count = frames.shape[0]
    radius = lax.broadcasted_iota(jnp.int32, (RADII, 2 * HARMONICS), 0)
    rows[...] = jnp.zeros_like(rows)
    for f in range(count):
        raw[f] = jnp.where(radius < lengths[f], frames[f].astype(jnp.float32), 0.0).astype(jnp.bfloat16)
        rows[f : f + 1, :] = jnp.full((1, 128), lengths[f].astype(jnp.float32))
    raw[count] = rows[...].astype(jnp.bfloat16)


def prepare_frames(lengths, frames):
    return pl.pallas_call(
        frames_kernel,
        out_shape=jax.ShapeDtypeStruct((frames.shape[0] + 1, RADII, 128), jnp.bfloat16),
        in_specs=[SMEM, VMEM],
        out_specs=VMEM,
        scratch_shapes=[pltpu.VMEM((RADII, 128), jnp.float32)],
        name="prepare_frames",
    )(lengths, frames)


def arrange_kernel(core, mine, theirs, out, scratch, rows):
    count = mine.shape[0] - 1
    both = 2 * count
    here = core[0] * count
    there = count - here
    for source, start in ((mine, here), (theirs, there)):
        for f in range(count):
            scratch[pl.ds(start + f, HARMONICS, stride=both + 1), :] = harmonic_rows(source[f].astype(jnp.float32))
        rows[pl.ds(start, count), :] = source[count].astype(jnp.float32)[0:count]
    for m in range(HARMONICS):
        out[m] = scratch[pl.ds(m * (both + 1), both), :].astype(jnp.bfloat16)
    out[HARMONICS] = rows[...].astype(jnp.bfloat16)


def arrange(core, mine, theirs):
    both = 2 * (mine.shape[0] - 1)
    return pl.pallas_call(
        arrange_kernel,
        out_shape=jax.ShapeDtypeStruct((HARMONICS + 1, both, 128), jnp.bfloat16),
        in_specs=[SMEM, VMEM, VMEM],
        out_specs=VMEM,
        scratch_shapes=[
            pltpu.VMEM((HARMONICS * (both + 1), 128), jnp.float32),
            pltpu.VMEM((both, 128), jnp.float32),
        ],
        name="arrange",
    )(core, mine, theirs)


def split(value):
    high = value.astype(jnp.bfloat16)
    return high, (value - high.astype(jnp.float32)).astype(jnp.bfloat16)


def dot(a, b):
    return jnp.dot(a, b, preferred_element_type=jnp.float32)


def project_kernel(harmonics, *refs):
    *pieces, high_out, low_out = refs
    ids = jnp.concatenate([ref[j, 0] for ref in pieces for j in range(ref.shape[0])], axis=0).astype(jnp.float32)
    bins = (ids[:, 0:1] * 32.0 + ids[:, 1:2]).astype(jnp.int32)
    onehot = (lax.broadcasted_iota(jnp.int32, (ids.shape[0], BINS), 1) == bins).astype(jnp.float32).astype(jnp.bfloat16)
    high, low = split(harmonics[...])
    high_out[...] = dot(onehot, high).astype(jnp.bfloat16)
    low_out[...] = dot(onehot, low).astype(jnp.bfloat16)


def project(harmonics, pieces):
    rows = sum(piece.shape[0] * piece.shape[2] for piece in pieces)
    shape = jax.ShapeDtypeStruct((rows, COEFS), jnp.bfloat16)
    spec = pl.BlockSpec((rows, COEFS), lambda i: (0, 0))
    return pl.pallas_call(
        project_kernel,
        grid=(1,),
        out_shape=(shape, shape),
        in_specs=[pl.BlockSpec((BINS, COEFS), lambda i: (0, 0))]
        + [pl.BlockSpec((p.shape[0], 1) + p.shape[2:], lambda i: (0, HARMONICS, 0, 0)) for p in pieces],
        out_specs=(spec, spec),
        compiler_params=pltpu.CompilerParams(vmem_limit_bytes=16 << 20),
        name="project",
    )(harmonics, *pieces)


def score_kernel(core, *refs, blocks, pieces, halves, chained, cut):
    frame_refs = refs[:blocks]
    piece_refs = refs[blocks : blocks + pieces]
    table = refs[blocks + pieces]
    refs = refs[blocks + pieces + 1 :]
    projections = refs[: 2 * halves]
    refs = refs[2 * halves :]
    before = refs[:chained]
    outs = refs[chained:-5]
    cross, per_template, turned, scale, reference = refs[-5:]
    size = frame_refs[0].shape[1]
    count = blocks * size
    tiles = 2 * halves

    def correlate(m, _):
        plain = jnp.concatenate([ref[m] for ref in frame_refs], axis=0).astype(jnp.float32)
        quarter = jnp.concatenate([plain[:, HARMONICS:], -plain[:, :HARMONICS]], axis=1)
        rows = jnp.concatenate([plain, quarter], axis=0).astype(jnp.bfloat16)
        columns = jnp.concatenate([ref[j, m] for ref in piece_refs for j in range(ref.shape[0])], axis=0)
        result = lax.dot_general(
            rows, columns, (((1,), (1,)), ((), ())), preferred_element_type=jnp.float32
        )
        for s in range(2):
            for j in range(tiles):
                cross[j, pl.ds(s * HARMONICS + m, count, stride=STRIDE), :] = result[
                    s * count : (s + 1) * count, j * 128 : (j + 1) * 128
                ]
        return 0

    lax.fori_loop(0, HARMONICS, correlate, 0, unroll=64)
    lengths = jnp.concatenate([ref[HARMONICS] for ref in frame_refs], axis=0).astype(jnp.float32)
    scale[...] = LOG2E / (8.0 * jnp.sqrt(lengths))
    lane = lax.broadcasted_iota(jnp.int32, (ANGLES, 128), 1)
    turned[...] = jnp.zeros_like(turned)

    def sums(f, exact):
        factor = scale[pl.ds(f, 1), :]
        factor = jnp.concatenate([factor] * 2, axis=1)

        def scored(h):
            spectra = jnp.concatenate(
                [cross[2 * h + j, pl.ds(f * STRIDE, 128), :].astype(jnp.bfloat16) for j in range(2)], axis=1
            )
            return dot(table[...], spectra) * factor

        if exact:
            tops = [jnp.max(scored(h), axis=(0, 1), keepdims=True) for h in range(halves)]
            top = functools.reduce(jnp.maximum, tops)
            reference[pl.ds(f, 1), :] = jnp.broadcast_to(top, (1, 128))
        across = None
        for h in range(halves):
            weights = jnp.exp2(scored(h) - top if exact else scored(h))
            per_template[pl.ds(f, 1), h * 256 : (h + 1) * 256] = jnp.sum(weights, axis=0, keepdims=True)
            folded = weights[:, :128] + weights[:, 128:]
            across = folded if across is None else across + folded
        turned[...] = jnp.where(lane == f, jnp.sum(across, axis=1, keepdims=True), turned[...])

    reference[...] = jnp.zeros_like(reference)
    for f in range(count):
        sums(f, False)
    totals = jnp.sum(per_template[...], axis=1, keepdims=True)
    safe = jnp.logical_and(jnp.max(totals) < 1e30, jnp.min(totals) > 1e-20)

    @pl.when(jnp.logical_not(safe))
    def _():
        lax.fori_loop(0, count, lambda f, _: (sums(f, True), 0)[1], 0)

    weights = per_template[...]
    totals = jnp.sum(weights, axis=1, keepdims=True)
    coefficients = None
    for h in range(halves):
        high, low = split(weights[:, h * 256 : (h + 1) * 256])
        high_ref, low_ref = projections[2 * h : 2 * h + 2]
        part = dot(high, high_ref[...]) + (dot(high, low_ref[...]) + dot(low, high_ref[...]))
        coefficients = part if coefficients is None else coefficients + part
    summary = jnp.concatenate(
        [
            coefficients,
            turned[...].T[:count],
            jnp.where(lax.broadcasted_iota(jnp.int32, (count, 128), 1) == 0, totals, reference[...]),
        ],
        axis=1,
    )
    if chained:
        groups = [before[i : i + blocks] for i in range(0, chained, blocks)]
        summary = merged([jnp.concatenate([ref[...] for ref in group], axis=0) for group in groups] + [summary])
    if cut:
        half = size // 2
        low, high = summary[:half], summary[half:]
        outs[0][...] = jnp.where(core[0] == 0, low, high)
        outs[1][...] = jnp.where(core[0] == 0, high, low)
    else:
        for block, out in enumerate(outs):
            out[...] = summary[block * size : (block + 1) * size]


def merged(summaries):
    references = [s[:, TOT + 1 : TOT + 2] for s in summaries]
    top = functools.reduce(jnp.maximum, references)
    total = None
    for s, r in zip(summaries, references):
        term = s * jnp.exp2(r - top)
        total = term if total is None else total + term
    column = lax.broadcasted_iota(jnp.int32, total.shape, 1)
    return jnp.where(column > TOT, top, total)


def score(core, frame_blocks, pieces, table, projections, before=(), cut=False):
    blocks, halves, size = len(frame_blocks), len(projections), frame_blocks[0].shape[1]
    count, templates = blocks * size, halves * 256
    operands = (*frame_blocks, *pieces, table, *sum(projections, ()), *before)
    pairs = count * templates
    out = jax.ShapeDtypeStruct((size // 2 if cut else size, WIDTH), jnp.float32)
    outs = 2 if cut else blocks
    return pl.pallas_call(
        functools.partial(
            score_kernel, blocks=blocks, pieces=len(pieces), halves=halves, chained=len(before), cut=cut
        ),
        out_shape=(out,) * outs,
        in_specs=[SMEM] + [VMEM] * len(operands),
        out_specs=(VMEM,) * outs,
        scratch_shapes=[
            pltpu.VMEM((templates // 128, count * STRIDE, 128), jnp.float32),
            pltpu.VMEM((count, templates), jnp.float32),
            pltpu.VMEM((ANGLES, 128), jnp.float32),
            pltpu.VMEM((count, 128), jnp.float32),
            pltpu.VMEM((count, 128), jnp.float32),
        ],
        compiler_params=pltpu.CompilerParams(vmem_limit_bytes=28 << 20),
        cost_estimate=pl.CostEstimate(
            flops=pairs * 65536 * 12, bytes_accessed=8 << 20, transcendentals=pairs * ANGLES
        ),
        name="score",
    )(core, *operands)


def finish_kernel(*refs):
    *summaries, coefficients, rotations = refs
    total = merged([ref[...] for ref in summaries])
    inverse = 1.0 / total[:, TOT : TOT + 1]
    coefficients[...] = total[:, :ROT] * inverse
    rotations[...] = total[:, ROT:TOT] * inverse


def finish(*summaries):
    count = summaries[0].shape[0]
    return pl.pallas_call(
        finish_kernel,
        out_shape=(
            jax.ShapeDtypeStruct((count, COEFS), jnp.float32),
            jax.ShapeDtypeStruct((count, ANGLES), jnp.float32),
        ),
        in_specs=[VMEM] * len(summaries),
        out_specs=(VMEM, VMEM),
        name="finish",
    )(*summaries)


def local(frames, lengths, templates, bin_ids, harmonics):
    core = (lax.axis_index("frames") % 2).reshape(1).astype(jnp.int32)
    table = rotation_table()
    raw = prepare_frames(lengths, frames)
    tmpl = prepare_templates(bin_ids, after(templates, raw))
    ahead = first_axis(tmpl, 1)
    behind = first_axis(tmpl, -1)
    opposite = first_axis(tmpl, 2)
    chip = arrange(core, raw, swap(raw))
    ahead, behind, opposite = after((ahead, behind, opposite), chip)
    ring1 = along_z(chip, 1)
    row1 = jnp.stack([tmpl, ahead])
    above1 = second_axis(row1, 1)
    below1 = second_axis(row1, -1)
    row2 = jnp.stack([behind, opposite])
    above2 = second_axis(row2, 1)
    below2 = second_axis(row2, -1)
    above1, below2 = after((above1, below2), ring1)
    far1 = second_axis(above1, 1)
    far2 = second_axis(below2, -1)
    ring2 = along_z(ring1, 1)
    ring3 = along_z(ring2, 1)
    own = (row1, row2, above1, below1, above2, below2, far1, far2)
    own_projection = project(harmonics, own)
    near = score(core, (ring1, ring2), own, table, (own_projection,))
    other = (
        swap(jnp.concatenate([row1, row2])),
        swap(jnp.concatenate([above1, below1])),
        swap(jnp.concatenate([above2, below2])),
        swap(jnp.concatenate([far1, far2])),
    )
    other = after(other, near[0])
    other_projection = project(harmonics, other)
    first, second = score(core, (ring1, ring2), other, table, (other_projection,), near)
    home1 = along_z(first, -1)
    home2 = along_z(second, -2)
    ring3 = after(ring3, second)
    ring4 = along_z(ring3, 1)
    (third,) = score(core, (ring3,), own + other, table, (own_projection, other_projection))
    home3 = along_z(third, -3)
    ring4 = after(ring4, third)
    fourth = score(core, (ring4,), own, table, (own_projection,), cut=True)
    home4 = go_home(*fourth, 4)
    chip = after(chip, fourth[0])
    keep, send = score(core, (chip,), own, table, (own_projection,), (home1, home2, home3), cut=True)
    send = after(send, home4)
    return finish(keep, swap(send), *home4)


def go_home(here, there, steps):
    return along_z(here, -steps), move(there, lambda core: (0, 0, -steps if core == 0 else steps, 1))


def solution(mesh):
    return jax.shard_map(
        local,
        mesh=mesh,
        in_specs=(
            P(AXES, None, None),
            P(AXES),
            P(AXES, None, None),
            P(AXES),
            P(),
        ),
        out_specs=(P(AXES, None), P(AXES, None)),
        check_vma=False,
    )
```
